32 devices in a mesh: dp: 4 (over z), shard: 8 (over y, x, core).
Axes of the slice: x: 2, y: 2, z: 4, core: 2. Of those that a mesh axis runs over, the one named last changes fastest.
Arguments:
- grad: bfloat16 [4, 4, 2, 1024, 8192], P('dp', None, None, 'shard'), may hold values from -6 to 6
- error: bfloat16 [4, 4, 2, 1024, 8192], P('dp', None, None, 'shard'), may hold values from -4 to 4
- q_prev: float32 [4, 2, 8, 8192], replicated, may hold values from -6 to 6
Outputs:
- error_out: bfloat16 [4, 4, 2, 1024, 8192], P('dp', None, None, 'shard')
- approx: float32 [4, 2, 1024, 8192], P(None, None, 'shard')
- q_new: float32 [4, 2, 8, 8192], replicated
The draws below stay inside these ranges and needn't reach their ends.
All inputs are finite; a program needn't handle non-finite values.
Results may differ from the reference program's by a relative error of at most 0.0014.
Values sent between devices are 32-bit elements; how exact they have to be, the bound alone decides.
No kernel may reach another device: no remote copies, remote signals or barrier semaphores. Data moves between devices by JAX's collectives and lax.ppermute only.
A program may use at most 192 MiB of HBM per device.

```python
import jax
import jax.numpy as jnp
from jax import lax

D = 8192
KV = 1024
LAYERS = 4
RANK = 8
N_DP = 4


def spiked(result, key, source, target, blocks, factor):
    owner, partner = [(jnp.arange(result.shape[dim]) // (result.shape[dim] // blocks)).reshape([-1 if axis == dim else 1 for axis in range(result.ndim)]) for dim in (source, target)]
    chosen = jax.random.permutation(key, blocks)[partner]
    strong = (owner == chosen) | (owner == (partner + blocks // 2) % blocks)
    return jnp.where(strong, factor * result, result)


def block_levels(key, dims, shards, smallest, top_value):
    gain = 1.0
    for axis_at, blocks in shards:
        heights = jax.random.uniform(jax.random.fold_in(jax.random.fold_in(key, 6), axis_at), (blocks,), jnp.float32, smallest / len(shards), top_value / len(shards))
        gain = gain * jnp.repeat(jnp.exp(heights), dims[axis_at] // blocks).reshape((-1,) + (1,) * (len(dims) - 1 - axis_at))
    return gain


def scatter_about(rng, shape, deviation, bound, pieces=(), dtype=jnp.bfloat16):
    values = deviation * jax.random.normal(rng, shape, jnp.float32)
    if pieces:
        values = values * block_levels(rng, shape, pieces, -0.22, 0.18)
    return jnp.clip(values, -bound, bound).astype(dtype)


def heavy_noise(own_key, dims, deviation, most, shards, heavy, dtype=jnp.bfloat16):
    values = deviation * jax.random.normal(own_key, dims, jnp.float32)
    if shards:
        values = values * block_levels(own_key, dims, shards, -0.22, 0.18)
    return jnp.clip(spiked(values, jax.random.fold_in(own_key, 3), *heavy), -most, most).astype(dtype)


def setup_inputs(seed: int = 0) -> dict:
    key_list = jax.random.split(jax.random.key(seed), 4)
    return {
        "grad": heavy_noise(key_list[0], (N_DP, LAYERS, 2, KV, D), 1.0, 6.0, ((0, 4), (3, 8)), (3, 4, 8, 2.0)),
        "error": scatter_about(key_list[1], (N_DP, LAYERS, 2, KV, D), 0.5, 4.0, ((0, 4), (3, 8))),
        "q_prev": scatter_about(key_list[2], (LAYERS, 2, RANK, D), 1.0, 6.0, (), jnp.float32),
    }


def reference(grad, error, q_prev):
    highest = lax.Precision.HIGHEST
    errors = []
    approxes = []
    factors = []
    for layer in range(LAYERS):
        for which in range(2):
            merged = grad[:, layer, which].astype(jnp.float32) + error[:, layer, which].astype(jnp.float32)
            basis = q_prev[layer, which]
            p_sum = jnp.einsum('grd,kd->rk', merged, basis, precision=highest)
            gram = jnp.einsum('rk,rj->kj', p_sum, p_sum, precision=highest)
            lower = jnp.linalg.cholesky(gram)
            p_orth = jax.scipy.linalg.solve_triangular(lower, p_sum.T, lower=True).T
            q_new = jnp.einsum('grd,rk->kd', merged, p_orth, precision=highest) / N_DP
            approx = jnp.einsum('rk,kd->rd', p_orth, q_new, precision=highest)
            errors.append((merged - approx[None]).astype(jnp.bfloat16))
            approxes.append(approx)
            factors.append(q_new)
    error_out = jnp.stack(errors, axis=1).reshape(grad.shape)
    approx_all = jnp.stack(approxes, axis=0).reshape(LAYERS, 2, KV, D)
    q_all = jnp.stack(factors, axis=0).reshape(LAYERS, 2, RANK, D)
    return (error_out, approx_all, q_all)
```

```python
import functools

import jax
import jax.numpy as jnp
from jax import lax
from jax.experimental import pallas as pl
from jax.experimental.pallas import tpu as pltpu
from jax.sharding import PartitionSpec as P

F32 = jnp.float32
BF16 = jnp.bfloat16
LANES = 128
MIB = 1 << 20


def split3(x):
    hi = x.astype(BF16).astype(F32)
    rest = x - hi
    mid = rest.astype(BF16).astype(F32)
    low = (rest - mid).astype(BF16).astype(F32)
    return hi, mid, low


def tree_sum(terms):
    terms = list(terms)
    while len(terms) > 1:
        terms = [terms[i] + terms[i + 1] for i in range(0, len(terms), 2)]
    return terms[0]


def left_kernel(g_hbm, e_hbm, q_hbm, g_out, e_out, p_out, q_in, sems, q_sem):
    matrices, rows, _ = g_out.shape
    rank = q_in.shape[1]

    def pair(m):
        return (
            pltpu.make_async_copy(g_hbm.at[m], g_out.at[m], sems.at[0, m]),
            pltpu.make_async_copy(e_hbm.at[m], e_out.at[m], sems.at[1, m]),
        )

    q_copy = pltpu.make_async_copy(q_hbm, q_in, q_sem)
    q_copy.start()
    for m in range(matrices):
        for copy in pair(m):
            copy.start()
    q_copy.wait()

    @pl.loop(0, matrices)
    def _(m):
        basis = jnp.concatenate(split3(q_in[m]), axis=0).astype(BF16)
        for copy in pair(m):
            copy.wait()
        both = jnp.concatenate([g_out[m], e_out[m]], axis=0)
        part = lax.dot_general(both, basis, (((1,), (1,)), ((), ())), preferred_element_type=F32)
        part = (part[:rows] + part[rows:]).T
        p_out[m] = part[:rank] + (part[rank : 2 * rank] + part[2 * rank :])


def right_kernel(me_ref, g_ref, e_ref, *refs, pieces, blocks):
    p_refs, (sum_out, gram_out, *outs), (left,) = refs[: -3 - blocks], refs[-3 - blocks : -1], refs[-1:]
    matrices, rows, width = g_ref.shape
    rank = sum_out.shape[1]
    p_sum = tree_sum([r[...] for r in p_refs])
    sum_out[...] = p_sum
    lane = lax.broadcasted_iota(jnp.int32, (rank, LANES), 1)
    gram = jnp.zeros((rank, LANES), F32)
    for m in range(matrices):
        one = p_sum[m]
        for j in range(rank):
            column = jnp.sum(one * one[j : j + 1], axis=1, keepdims=True)
            gram = jnp.where(lane == j * matrices + m, column, gram)
        terms = jnp.concatenate(split3(one), axis=0)
        left[m] = jnp.concatenate([terms, terms], axis=1).astype(BF16)
    gram_out[...] = gram
    me = me_ref[0]
    per = pieces // matrices
    columns = width // per
    each = pieces // blocks

    for block in range(blocks):

        @pl.loop(0, each)
        def _(slot):
            piece = jnp.bitwise_xor(slot + block * each, me)
            m = piece // per
            start = pl.multiple_of(lax.rem(piece, per) * columns, columns)
            both = jnp.concatenate(
                [g_ref[m, :, pl.ds(start, columns)], e_ref[m, :, pl.ds(start, columns)]], axis=0
            )
            part = jnp.dot(left[m], both, preferred_element_type=F32)
            part = part[:rank] + (part[rank : 2 * rank] + part[2 * rank :])
            for t in range(columns // LANES):
                outs[block][slot, t] = part[:, t * LANES : (t + 1) * LANES]


def invert(gram, matrices, rank):
    row = lax.broadcasted_iota(jnp.int32, (rank, LANES), 0)
    lane = lax.broadcasted_iota(jnp.int32, (rank, LANES), 1)
    used = lane < matrices
    unit = [jnp.where(row == j, 1.0, 0.0).astype(F32) for j in range(rank)]
    cols = [
        jnp.where(used, gram if j == 0 else pltpu.roll(gram, LANES - j * matrices, 1), unit[j]) for j in range(rank)
    ]
    inverse = list(unit)
    scale = jnp.ones((rank, LANES), F32)
    for k in range(rank):
        pivot = jnp.broadcast_to(cols[k][k : k + 1], (rank, LANES))
        scale = jnp.where(row == k, 1.0 / jnp.sqrt(pivot), scale)
        factor = jnp.where(row > k, cols[k] / pivot, 0.0)
        for j in range(k + 1, rank):
            cols[j] = cols[j] - factor * cols[j][k : k + 1]
        for j in range(k + 1):
            inverse[j] = inverse[j] - factor * inverse[j][k : k + 1]
    return [scale * c for c in inverse]


def piece_kernel(me_ref, gram_ref, *refs, pieces, matrices, groups):
    part_refs, (q_out, inv_out) = refs[:-2], refs[-2:]
    rank = gram_ref.shape[0]
    inverse = invert(gram_ref[...], matrices, rank)
    for j in range(rank):
        inv_out[j] = inverse[j]
    m = me_ref[0] // (pieces // matrices)
    lane = lax.broadcasted_iota(jnp.int32, (rank, LANES), 1)
    picked = [
        jnp.broadcast_to(jnp.sum(jnp.where(lane == m, c, 0.0), axis=1, keepdims=True), (rank, LANES)) / groups
        for c in inverse
    ]
    for t in range(q_out.shape[0]):
        total = tree_sum([r[t] for r in part_refs])
        q_out[t] = sum(picked[j] * total[j : j + 1] for j in range(rank))


def out_kernel(me_ref, g_ref, e_ref, sum_ref, inv_ref, *refs, pieces, splits):
    q_refs, (err_out, approx_out, q_out, p_left) = refs[:-4], refs[-4:]
    m = pl.program_id(0)
    part = pl.program_id(1)
    matrices, rows, width = g_ref.shape
    rank = sum_ref.shape[1]
    per = pieces // matrices
    columns = width // per
    each = pieces // len(q_refs)

    @pl.when((m == 0) & (part == 0))
    def _():
        for block, ref in enumerate(q_refs):

            @pl.loop(0, each)
            def _(slot):
                piece = jnp.bitwise_xor(slot + block * each, me_ref[0])
                start = pl.multiple_of(lax.rem(piece, per) * columns, columns)
                for t in range(columns // LANES):
                    q_out[piece // per, :, pl.ds(start + t * LANES, LANES)] = ref[slot, t]

    @pl.when(part == 0)
    def _():
        lane = lax.broadcasted_iota(jnp.int32, (rank, LANES), 1)
        one = sum_ref[m]
        orth = jnp.zeros((rank, rows), F32)
        for j in range(rank):
            weight = jnp.sum(jnp.where(lane == m, inv_ref[j], 0.0), axis=1, keepdims=True)
            orth = orth + weight * one[j : j + 1]
        hi = orth.astype(BF16).astype(F32)
        low = (orth - hi).astype(BF16).astype(F32)
        p_left[...] = jnp.concatenate([hi, low, hi], axis=0).T.astype(BF16)

    step = min(columns, width // splits)
    for k in range(width // splits // step):
        start = pl.multiple_of(part * (width // splits) + k * step, step)
        right = q_out[m, :, pl.ds(start, step)]
        hi = right.astype(BF16).astype(F32)
        low = (right - hi).astype(BF16).astype(F32)
        terms = jnp.concatenate([hi, hi, low], axis=0).astype(BF16)
        approx = jnp.dot(p_left[...], terms, preferred_element_type=F32)
        here = pl.ds(k * step, step)
        approx_out[0, :, here] = approx
        merged = g_ref[m, :, pl.ds(start, step)].astype(F32) + e_ref[m, :, pl.ds(start, step)].astype(F32)
        err_out[0, :, here] = (merged - approx).astype(BF16)


def on_device(sizes, grad, error, q_prev):
    groups, shards = sizes
    _, layers, pair, rows, width = grad.shape
    matrices = layers * pair
    rank = q_prev.shape[2]
    pieces = groups * shards
    chips = shards // 2
    stages = [("shard", 1, 2)]
    step = 2
    while chips > 1:
        count = min(4, chips)
        stages.append(("shard", step, count))
        step, chips = step * count, chips // count
    stages.append(("dp", 1, groups))
    me = jnp.int32(0)
    for name, step, count in stages:
        me = me * count + (lax.axis_index(name) // step) % count
    me = me.reshape(1)
    tiles = matrices * width // pieces // LANES

    vmem = pl.BlockSpec(memory_space=pltpu.VMEM)
    smem = pl.BlockSpec(memory_space=pltpu.SMEM)
    anywhere = pl.BlockSpec(memory_space=pl.ANY)

    def swap(x, name, step, k):
        size = sizes[0] if name == "dp" else sizes[1]
        return lax.ppermute(x, name, [(i, i ^ (k * step)) for i in range(size)])

    def pinned(x):
        return pltpu.with_memory_space_constraint(x, pltpu.VMEM)

    block = (matrices, rows, width)
    g_keep, e_keep, p_own = pl.pallas_call(
        left_kernel,
        out_shape=(
            pltpu.VMEM(block, BF16),
            pltpu.VMEM(block, BF16),
            jax.ShapeDtypeStruct((matrices, rank, rows), F32),
        ),
        in_specs=[anywhere] * 3,
        out_specs=(vmem, vmem, vmem),
        scratch_shapes=[
            pltpu.VMEM((matrices, rank, width), F32),
            pltpu.SemaphoreType.DMA((2, matrices)),
            pltpu.SemaphoreType.DMA,
        ],
        compiler_params=pltpu.CompilerParams(vmem_limit_bytes=8 * MIB),
        name="left",
    )(grad.reshape(block), error.reshape(block), q_prev.reshape(matrices, rank, width))

    p_all = [p_own] + [swap(p_own, "dp", 1, k) for k in range(1, groups)]

    each = pieces // 2
    p_sum, gram, *halves = pl.pallas_call(
        functools.partial(right_kernel, pieces=pieces, blocks=2),
        out_shape=(
            jax.ShapeDtypeStruct((matrices, rank, rows), F32),
            jax.ShapeDtypeStruct((rank, LANES), F32),
        )
        + (jax.ShapeDtypeStruct((each, tiles, rank, LANES), F32),) * 2,
        in_specs=[smem] + [vmem] * (2 + groups),
        out_specs=(vmem,) * 4,
        scratch_shapes=[pltpu.VMEM((matrices, 3 * rank, 2 * rows), BF16)],
        compiler_params=pltpu.CompilerParams(vmem_limit_bytes=10 * MIB),
        name="right",
    )(me, pinned(g_keep), pinned(e_keep), *p_all)

    for at, (name, step, count) in enumerate(stages):
        arrived = [swap(halves[k], name, step, k) for k in range(1, count)]
        if name == "shard":
            gram = tree_sum([gram] + [swap(gram, name, step, k) for k in range(1, count)])
        if at < len(stages) - 1:
            following = stages[at + 1][2]
            each //= following
            shape = (following, each, tiles, rank, LANES)
            terms = [x.reshape(shape) for x in [halves[0]] + arrived]
            halves = [tree_sum([x[k] for x in terms]) for k in range(following)]
    parts = [x.reshape(tiles, rank, LANES) for x in [halves[0]] + arrived]

    piece, inverse = pl.pallas_call(
        functools.partial(piece_kernel, pieces=pieces, matrices=matrices, groups=groups),
        out_shape=(
            jax.ShapeDtypeStruct((tiles, rank, LANES), F32),
            jax.ShapeDtypeStruct((rank, rank, LANES), F32),
        ),
        in_specs=[smem] + [vmem] * (1 + groups),
        out_specs=(vmem, vmem),
        compiler_params=pltpu.CompilerParams(vmem_limit_bytes=4 * MIB),
        name="piece",
    )(me, gram, *parts)

    ready = [piece.reshape(1, tiles, rank, LANES)]
    for name, step, count in reversed(stages):
        ready = ready + [swap(x, name, step, k) for k in range(1, count) for x in ready]
        if name == "dp":
            ready = [jnp.concatenate(ready, axis=0)]

    splits = 2
    out_block = (1, rows, width // splits)

    def whole_spec(space):
        return pl.BlockSpec(memory_space=space)

    error_out, approx, q_new = pl.pallas_call(
        functools.partial(out_kernel, pieces=pieces, splits=splits),
        grid=(matrices, splits),
        out_shape=(
            jax.ShapeDtypeStruct(block, BF16),
            jax.ShapeDtypeStruct(block, F32),
            jax.ShapeDtypeStruct((matrices, rank, width), F32),
        ),
        in_specs=[smem] + [vmem] * (4 + len(ready)),
        out_specs=(
            pl.BlockSpec(out_block, lambda m, s: (m, 0, s)),
            pl.BlockSpec(out_block, lambda m, s: (m, 0, s)),
            vmem,
        ),
        scratch_shapes=[pltpu.VMEM((rows, 3 * rank), BF16)],
        compiler_params=pltpu.CompilerParams(
            vmem_limit_bytes=16 * MIB, dimension_semantics=("arbitrary", "arbitrary")
        ),
        name="out",
    )(me, pinned(g_keep), pinned(e_keep), p_sum, inverse, *ready)
    return error_out.reshape(grad.shape), approx.reshape(layers, pair, rows, width), q_new.reshape(q_prev.shape)


def solution(mesh):
    sizes = (mesh.shape["dp"], mesh.shape["shard"])
    in_specs = (P("dp", None, None, "shard", None), P("dp", None, None, "shard", None), P())
    out_specs = (P("dp", None, None, "shard", None), P(None, None, "shard", None), P())
    return jax.shard_map(
        functools.partial(on_device, sizes), mesh=mesh, in_specs=in_specs, out_specs=out_specs, check_vma=False
    )
```

```python
import functools

import jax
import jax.numpy as jnp
from jax import lax
from jax.experimental import pallas as pl
from jax.experimental.pallas import tpu as pltpu
from jax.sharding import PartitionSpec as P

F32 = jnp.float32
BF16 = jnp.bfloat16
LANES = 128
MIB = 1 << 20


def split3(x):
    hi = x.astype(BF16).astype(F32)
    rest = x - hi
    mid = rest.astype(BF16).astype(F32)
    low = (rest - mid).astype(BF16).astype(F32)
    return hi, mid, low


def tree_sum(terms):
    terms = list(terms)
    while len(terms) > 1:
        terms = [terms[i] + terms[i + 1] for i in range(0, len(terms), 2)]
    return terms[0]


def left_kernel(g_ref, e_ref, q_ref, p_out, total, *, splits):
    part = pl.program_id(1)
    rows = g_ref.shape[1]
    rank = q_ref.shape[1]
    basis = jnp.concatenate(split3(q_ref[0]), axis=0).astype(BF16)
    both = jnp.concatenate([g_ref[0], e_ref[0]], axis=0)
    here = lax.dot_general(both, basis, (((1,), (1,)), ((), ())), preferred_element_type=F32)

    @pl.when(part == 0)
    def _():
        total[...] = here

    @pl.when(part > 0)
    def _():
        total[...] += here

    @pl.when(part == splits - 1)
    def _():
        whole = (total[:rows] + total[rows:]).T
        p_out[0] = whole[:rank] + (whole[rank : 2 * rank] + whole[2 * rank :])


def right_kernel(core_ref, g_ref, e_ref, *refs, flip, splits):
    p_refs, (sum_out, out, left) = refs[:-3], refs[-3:]
    i = pl.program_id(0)
    part = pl.program_id(1)
    count, rank, _ = sum_out.shape
    half = out.shape[0] - 1
    tiles = g_ref.shape[2] // LANES

    @pl.when((i == 0) & (part == 0))
    def _():
        p_sum = tree_sum([r[...] for r in p_refs])
        sum_out[...] = p_sum
        lane = lax.broadcasted_iota(jnp.int32, (rank, LANES), 1)
        gram = jnp.zeros((rank, LANES), F32)
        for m in range(count):
            one = p_sum[m]
            for j in range(rank):
                column = jnp.sum(one * one[j : j + 1], axis=1, keepdims=True)
                gram = jnp.where(lane == j * count + m, column, gram)
            terms = jnp.concatenate(split3(one), axis=0)
            left[m] = jnp.concatenate([terms, terms], axis=1).astype(BF16)
        out[half] = gram

    m = jnp.bitwise_xor(core_ref[0], flip) * (count // 2) + i
    both = jnp.concatenate([g_ref[0], e_ref[0]], axis=0)
    product = jnp.dot(left[m], both, preferred_element_type=F32)
    product = product[:rank] + (product[rank : 2 * rank] + product[2 * rank :])
    first = (i * splits + part) * tiles
    for t in range(tiles):
        out[first + t] = product[:, t * LANES : (t + 1) * LANES]


def fold_kernel(at_ref, *refs, count, extra):
    terms, outs = refs[: len(refs) - count - extra], refs[len(refs) - count - extra :]
    size = terms[0].shape[0] - 1
    each = size // count
    last = tree_sum([r[size] for r in terms])
    for k in range(count):
        start = pl.multiple_of(jnp.bitwise_xor(at_ref[0], k) * each, each)
        here = pl.ds(start, each)
        outs[k][:each] = tree_sum([r[here] for r in terms])
        if not extra:
            outs[k][each] = last
    if extra:
        outs[count][...] = last


def join_kernel(at_ref, *refs):
    pieces, out = refs[:-1], refs[-1]
    each = pieces[0].shape[0]
    for k, piece in enumerate(pieces):
        start = pl.multiple_of(jnp.bitwise_xor(at_ref[0], k) * each, each)
        out[pl.ds(start, each)] = piece[...]


def invert(gram, matrices, rank):
    row = lax.broadcasted_iota(jnp.int32, (rank, LANES), 0)
    lane = lax.broadcasted_iota(jnp.int32, (rank, LANES), 1)
    used = lane < matrices
    unit = [jnp.where(row == j, 1.0, 0.0).astype(F32) for j in range(rank)]
    cols = [
        jnp.where(used, gram if j == 0 else pltpu.roll(gram, LANES - j * matrices, 1), unit[j]) for j in range(rank)
    ]
    inverse = list(unit)
    scale = jnp.ones((rank, LANES), F32)
    for k in range(rank):
        pivot = jnp.broadcast_to(cols[k][k : k + 1], (rank, LANES))
        scale = jnp.where(row == k, 1.0 / jnp.sqrt(pivot), scale)
        factor = jnp.where(row > k, cols[k] / pivot, 0.0)
        for j in range(k + 1, rank):
            cols[j] = cols[j] - factor * cols[j][k : k + 1]
        for j in range(k + 1):
            inverse[j] = inverse[j] - factor * inverse[j][k : k + 1]
    return [scale * c for c in inverse]


def piece_kernel(at_ref, gram_ref, *refs, per, matrices):
    parts, (q_out, inv_out) = refs[:-2], refs[-2:]
    rank = gram_ref.shape[0]
    inverse = invert(gram_ref[...], matrices, rank)
    for j in range(rank):
        inv_out[j] = inverse[j]
    m = at_ref[0] // per
    lane = lax.broadcasted_iota(jnp.int32, (rank, LANES), 1)
    picked = [
        jnp.broadcast_to(jnp.sum(jnp.where(lane == m, c, 0.0), axis=1, keepdims=True), (rank, LANES)) / len(parts)
        for c in inverse
    ]
    for t in range(q_out.shape[0]):
        total = tree_sum([r[t] for r in parts])
        q_out[t] = sum(picked[j] * total[j : j + 1] for j in range(rank))


def out_kernel(core_ref, g_ref, e_ref, sum_ref, inv_ref, q_ref, *refs, flip):
    err_out, approx_out, q_out, token, left = refs[-5:]
    i = pl.program_id(0)
    rows, width = g_ref.shape[1:]
    count, rank, _ = sum_ref.shape

    @pl.when(pl.program_id(1) == 0)
    def _():
        m = jnp.bitwise_xor(core_ref[0], flip) * (count // 2) + i
        lane = lax.broadcasted_iota(jnp.int32, (rank, LANES), 1)
        one = sum_ref[m]
        orth = jnp.zeros((rank, rows), F32)
        for j in range(rank):
            weight = jnp.sum(jnp.where(lane == m, inv_ref[j], 0.0), axis=1, keepdims=True)
            orth = orth + weight * one[j : j + 1]
        hi = orth.astype(BF16).astype(F32)
        low = (orth - hi).astype(BF16).astype(F32)
        left[...] = jnp.concatenate([hi, low, hi], axis=0).T.astype(BF16)
        token[...] = inv_ref[0]

    step = min(width, 1024)
    for start in range(0, width, step):
        here = slice(start, start + step)
        right = jnp.concatenate([q_ref[t] for t in range(start // LANES, (start + step) // LANES)], axis=1)
        q_out[0, :, here] = right
        hi = right.astype(BF16).astype(F32)
        low = (right - hi).astype(BF16).astype(F32)
        terms = jnp.concatenate([hi, hi, low], axis=0).astype(BF16)
        approx = jnp.dot(left[...], terms, preferred_element_type=F32)
        approx_out[0, :, here] = approx
        merged = g_ref[0, :, here].astype(F32) + e_ref[0, :, here].astype(F32)
        err_out[0, :, here] = (merged - approx).astype(BF16)


VMEM = pl.BlockSpec(memory_space=pltpu.VMEM)
HBM = pl.BlockSpec(memory_space=pltpu.HBM)
SMEM = pl.BlockSpec(memory_space=pltpu.SMEM)
ANY = pl.BlockSpec(memory_space=pl.ANY)
CHUNKS = 2
LEFT_SPLITS = 2
RIGHT_SPLITS = 2
OUT_SPLITS = 4


def ordered(kernel, count, at=0):
    def call(*refs):
        kernel(*refs[:at], *refs[at + count :])

    return call


def limit(mib, **more):
    return pltpu.CompilerParams(vmem_limit_bytes=mib * MIB, **more)


def cost(moved, flops=0):
    return pl.CostEstimate(flops=flops, bytes_accessed=moved // 4, transcendentals=0)


def on_device(sizes, grad, error, q_prev):
    groups, shards = sizes
    _, layers, pair, rows, width = grad.shape
    matrices = layers * pair
    rank = q_prev.shape[2]
    plane = shards // 2
    pieces = groups * shards
    whole = (matrices, rows, width)
    count = matrices // CHUNKS
    half = count // 2 * width // LANES
    tiles = half // (plane * groups)
    in_bytes = 4 * rows * width
    out_bytes = in_bytes + 6 * rows * width

    shard = lax.axis_index("shard")
    core = lax.rem(shard, 2).reshape(1)
    chip = (shard // 2).reshape(1)
    group = lax.axis_index("dp").reshape(1)
    at = (core * plane + chip) * groups + group

    grads, errors, basis = [
        pltpu.with_memory_space_constraint(x, pltpu.HBM)
        for x in (grad.reshape(whole), error.reshape(whole), q_prev.reshape(matrices, rank, width))
    ]

    def tiled(*shape):
        return jax.ShapeDtypeStruct(shape + (rank, LANES), F32)

    def swap(x, name, k):
        size = sizes[0] if name == "dp" else sizes[1]
        return lax.ppermute(x, name, [(i, i ^ k) for i in range(size)])

    def small(kernel, out_shape, *args, name, after=()):
        return pl.pallas_call(
            ordered(kernel, len(after)),
            out_shape=out_shape,
            in_specs=[ANY] * len(after) + [SMEM] + [VMEM] * (len(args) - 1),
            out_specs=jax.tree.map(lambda _: VMEM, out_shape),
            compiler_params=limit(16),
            name=name,
        )(*after, *args)

    def left(first):
        wide = width // LEFT_SPLITS
        block = pl.BlockSpec((1, rows, wide), lambda m, s: (first + m, 0, s))
        return pl.pallas_call(
            functools.partial(left_kernel, splits=LEFT_SPLITS),
            grid=(count, LEFT_SPLITS),
            out_shape=jax.ShapeDtypeStruct((count, rank, rows), F32),
            in_specs=[block, block, pl.BlockSpec((1, rank, wide), lambda m, s: (first + m, 0, s))],
            out_specs=pl.BlockSpec((1, rank, rows), lambda m, s: (m, 0, 0)),
            scratch_shapes=[pltpu.VMEM((2 * rows, 3 * rank), F32)],
            compiler_params=limit(24, dimension_semantics=("arbitrary",) * 2),
            cost_estimate=cost(count * (in_bytes + 4 * rank * width)),
            name="left",
        )(grads, errors, basis)

    def right(first, flip, parts, after):
        wide = width // RIGHT_SPLITS
        block = pl.BlockSpec(
            (1, rows, wide), lambda m, s, core: (first + jnp.bitwise_xor(core[0], flip) * (count // 2) + m, 0, s)
        )
        return pl.pallas_call(
            ordered(functools.partial(right_kernel, flip=flip, splits=RIGHT_SPLITS), len(after), 1),
            out_shape=(jax.ShapeDtypeStruct((count, rank, rows), F32), tiled(half + 1)),
            grid_spec=pltpu.PrefetchScalarGridSpec(
                num_scalar_prefetch=1,
                grid=(count // 2, RIGHT_SPLITS),
                in_specs=[ANY] * len(after) + [block, block] + [VMEM] * groups,
                out_specs=(VMEM, VMEM),
                scratch_shapes=[pltpu.VMEM((count, 3 * rank, 2 * rows), BF16)],
            ),
            compiler_params=limit(24, dimension_semantics=("arbitrary",) * 2),
            cost_estimate=cost(count // 2 * in_bytes),
            name="right",
        )(core, *after, grads, errors, *parts)

    def out(first, flip, p_sum, inverse, right_factors, before, after):
        wide = width // OUT_SPLITS

        def place(m, s, core):
            return (first + jnp.bitwise_xor(core[0], flip) * (count // 2) + m, 0, s)

        block = pl.BlockSpec((1, rows, wide), place)
        return pl.pallas_call(
            ordered(functools.partial(out_kernel, flip=flip), len(after), 1),
            out_shape=(
                jax.ShapeDtypeStruct(whole, BF16),
                jax.ShapeDtypeStruct(whole, F32),
                jax.ShapeDtypeStruct((matrices, rank, width), F32),
                tiled(),
            ),
            grid_spec=pltpu.PrefetchScalarGridSpec(
                num_scalar_prefetch=1,
                grid=(count // 2, OUT_SPLITS),
                in_specs=[ANY] * len(after)
                + [block, block, VMEM, VMEM]
                + [pl.BlockSpec((wide // LANES, rank, LANES), lambda m, s, core: (m * OUT_SPLITS + s, 0, 0))]
                + [HBM] * len(before),
                out_specs=(block, block, pl.BlockSpec((1, rank, wide), place), VMEM),
                scratch_shapes=[pltpu.VMEM((rows, 3 * rank), BF16)],
            ),
            input_output_aliases={6 + len(after) + k: k for k in range(len(before))},
            compiler_params=limit(24, dimension_semantics=("arbitrary",) * 2),
            cost_estimate=cost(count // 2 * out_bytes),
            name="out",
        )(core, *after, grads, errors, p_sum, inverse, right_factors, *before)

    def spread(x, name, step, size):
        return [x] + [swap(x, name, k * step) for k in range(1, size)]

    def exchange(parts, name, step):
        return [parts[0]] + [swap(x, name, k * step) for k, x in enumerate(parts) if k]

    chunks = range(CHUNKS)
    starts = [c * count for c in chunks]
    own = [left(first) for first in starts]
    lefts = [spread(x, "dp", 1, groups) for x in own]
    sums, keeps, messages = [], [], []
    before = own[1:2]
    for c in chunks:
        p_sum, send = right(starts[c], 1, lefts[c], before)
        arrived = swap(send, "shard", 1)
        _, keep = right(starts[c], 0, lefts[c], [p_sum])
        sums.append(p_sum)
        keeps.append(keep)
        messages.append(
            small(
                functools.partial(fold_kernel, count=plane, extra=0),
                (tiled(half // plane + 1),) * plane,
                chip, keep, arrived, name="fold_plane",
            )
        )
        before = messages[-1][:1]
    def group_stage(c, after):
        *parts, gram = small(
            functools.partial(fold_kernel, count=groups, extra=1),
            (tiled(tiles),) * groups + (tiled(),),
            group, *exchange(messages[c], "shard", 2), name="fold_group", after=after,
        )
        return parts, gram

    folded = [group_stage(0, keeps[1:2])]
    inverses, rows_here, pieces_made = [], [], []
    before = [x[0] for x in messages[1:2]]
    for c in chunks:
        parts, gram = folded[c]
        piece, inverse = small(
            functools.partial(piece_kernel, per=pieces // count, matrices=count),
            (tiled(tiles), tiled(rank)),
            at, gram, *exchange(parts, "dp", 1), name="piece", after=before,
        )
        pieces_made.append(piece)
        if c + 1 < CHUNKS:
            folded.append(group_stage(c + 1, [piece]))
        before = [x[0][0] for x in folded[c + 1 : c + 2]]
        row = small(
            join_kernel, tiled(tiles * groups), group, *spread(piece, "dp", 1, groups), name="join_group", after=before
        )
        before = [row]
        inverses.append(inverse)
        rows_here.append(spread(row, "shard", 2, plane))
    results, done = (), pieces_made[1:2]
    for c in chunks:
        mine = small(join_kernel, tiled(half), chip, *rows_here[c], name="join_plane", after=done)
        following = [x[0] for x in rows_here[c + 1 : c + 2]]
        for flip, factors in enumerate((mine, swap(mine, "shard", 1))):
            *results, token = out(starts[c], flip, sums[c], inverses[c], factors, results, following)
            following, done = [], [token]
    error_out, approx, q_new = results
    return error_out.reshape(grad.shape), approx.reshape(layers, pair, rows, width), q_new.reshape(q_prev.shape)


def solution(mesh):
    sizes = (mesh.shape["dp"], mesh.shape["shard"])
    in_specs = (P("dp", None, None, "shard", None), P("dp", None, None, "shard", None), P())
    out_specs = (P("dp", None, None, "shard", None), P(None, None, "shard", None), P())
    return jax.shard_map(
        functools.partial(on_device, sizes), mesh=mesh, in_specs=in_specs, out_specs=out_specs, check_vma=False
    )
```

```python
import functools

import jax
import jax.numpy as jnp
from jax import lax
from jax.experimental import pallas as pl
from jax.experimental.pallas import tpu as pltpu
from jax.sharding import PartitionSpec as P

F32 = jnp.float32
BF16 = jnp.bfloat16
LANES = 128
MIB = 1 << 20


def split3(x):
    hi = x.astype(BF16).astype(F32)
    rest = x - hi
    mid = rest.astype(BF16).astype(F32)
    low = (rest - mid).astype(BF16).astype(F32)
    return hi, mid, low


def tree_sum(terms):
    terms = list(terms)
    while len(terms) > 1:
        terms = [terms[i] + terms[i + 1] for i in range(0, len(terms), 2)]
    return terms[0]


def left_kernel(g_hbm, e_hbm, q_hbm, both_out, p_out, q_in, sems, *, first):
    count, height, _ = both_out.shape
    rows = height // 2
    rank = q_in.shape[1]

    def fetch(i):
        return (
            pltpu.make_async_copy(q_hbm.at[first + i], q_in.at[i], sems.at[0, i]),
            pltpu.make_async_copy(g_hbm.at[first + i], both_out.at[i, pl.ds(0, rows)], sems.at[1, i]),
            pltpu.make_async_copy(e_hbm.at[first + i], both_out.at[i, pl.ds(rows, rows)], sems.at[2, i]),
        )

    for i in range(count):
        for copy in fetch(i):
            copy.start()

    @pl.loop(0, count)
    def _(i):
        for copy in fetch(i):
            copy.wait()
        basis = jnp.concatenate(split3(q_in[i]), axis=0).astype(BF16)
        part = lax.dot_general(both_out[i], basis, (((1,), (1,)), ((), ())), preferred_element_type=F32)
        part = (part[:rows] + part[rows:]).T
        p_out[i] = part[:rank] + (part[rank : 2 * rank] + part[2 * rank :])


def add_kernel(a_ref, b_ref, out):
    out[...] = a_ref[...] + b_ref[...]


def right_kernel(at_ref, both_ref, *refs):
    p_refs, (sum_out, keep_out, send_out, left) = refs[:-4], refs[-4:]
    count, rank, _ = sum_out.shape
    width = both_ref.shape[2]
    p_sum = tree_sum([r[...] for r in p_refs])
    sum_out[...] = p_sum
    lane = lax.broadcasted_iota(jnp.int32, (rank, LANES), 1)
    gram = jnp.zeros((rank, LANES), F32)
    for m in range(count):
        one = p_sum[m]
        for j in range(rank):
            column = jnp.sum(one * one[j : j + 1], axis=1, keepdims=True)
            gram = jnp.where(lane == j * count + m, column, gram)
        terms = jnp.concatenate(split3(one), axis=0)
        left[m] = jnp.concatenate([terms, terms], axis=1).astype(BF16)
    core = at_ref[0]
    half = keep_out.shape[0] - 1
    step = min(width, 2048)
    per = width // step
    tiles = step // LANES
    for out, mine in ((send_out, 1 - core), (keep_out, core)):
        out[half] = gram

        @pl.loop(0, count // 2 * per)
        def _(at):
            m = mine * (count // 2) + at // per
            start = pl.multiple_of(lax.rem(at, per) * step, step)
            part = jnp.dot(left[m], both_ref[m, :, pl.ds(start, step)], preferred_element_type=F32)
            part = part[:rank] + (part[rank : 2 * rank] + part[2 * rank :])
            for t in range(tiles):
                out[at * tiles + t] = part[:, t * LANES : (t + 1) * LANES]


def fold_kernel(at_ref, a_ref, b_ref, keep_out, send_out, *last_out):
    each = a_ref.shape[0] // 2
    for out, mine in ((send_out, 1 - at_ref[0]), (keep_out, at_ref[0])):
        here = pl.ds(pl.multiple_of(mine * each, each), each)
        out[pl.ds(0, each)] = a_ref[here] + b_ref[here]
    if a_ref.shape[0] % 2:
        last = a_ref[2 * each] + b_ref[2 * each]
        if last_out:
            last_out[0][...] = last
        else:
            keep_out[each] = last
            send_out[each] = last


def join_kernel(at_ref, mine_ref, other_ref, out):
    each = mine_ref.shape[0]
    out[pl.ds(pl.multiple_of(at_ref[0] * each, each), each)] = mine_ref[...]
    out[pl.ds(pl.multiple_of((1 - at_ref[0]) * each, each), each)] = other_ref[...]


def invert(gram, matrices, rank):
    row = lax.broadcasted_iota(jnp.int32, (rank, LANES), 0)
    lane = lax.broadcasted_iota(jnp.int32, (rank, LANES), 1)
    used = lane < matrices
    unit = [jnp.where(row == j, 1.0, 0.0).astype(F32) for j in range(rank)]
    cols = [
        jnp.where(used, gram if j == 0 else pltpu.roll(gram, LANES - j * matrices, 1), unit[j]) for j in range(rank)
    ]
    inverse = list(unit)
    scale = jnp.ones((rank, LANES), F32)
    for k in range(rank):
        pivot = jnp.broadcast_to(cols[k][k : k + 1], (rank, LANES))
        scale = jnp.where(row == k, 1.0 / jnp.sqrt(pivot), scale)
        factor = jnp.where(row > k, cols[k] / pivot, 0.0)
        for j in range(k + 1, rank):
            cols[j] = cols[j] - factor * cols[j][k : k + 1]
        for j in range(k + 1):
            inverse[j] = inverse[j] - factor * inverse[j][k : k + 1]
    return [scale * c for c in inverse]


def piece_kernel(at_ref, gram_ref, a_ref, b_ref, q_out, inv_out, *, per, groups, matrices):
    rank = gram_ref.shape[0]
    inverse = invert(gram_ref[...], matrices, rank)
    for j in range(rank):
        inv_out[j] = inverse[j]
    m = at_ref[0] // per
    lane = lax.broadcasted_iota(jnp.int32, (rank, LANES), 1)
    picked = [
        jnp.broadcast_to(jnp.sum(jnp.where(lane == m, c, 0.0), axis=1, keepdims=True), (rank, LANES)) / groups
        for c in inverse
    ]
    for t in range(q_out.shape[0]):
        total = a_ref[t] + b_ref[t]
        q_out[t] = sum(picked[j] * total[j : j + 1] for j in range(rank))


def out_kernel(at_ref, both_ref, sum_ref, inv_ref, q_ref, *refs, first, flip):
    err_hbm, approx_hbm, q_hbm, token, q_buf, err_buf, approx_buf, left, sems, q_sems = refs[-10:]
    count, rank, rows = sum_ref.shape
    width = both_ref.shape[2]
    slots, _, step = err_buf.shape
    tiles = step // LANES
    per = width // step
    total = count // 2 * per
    base = jnp.bitwise_xor(at_ref[0], flip) * (count // 2)
    token[...] = inv_ref[0]
    lane = lax.broadcasted_iota(jnp.int32, (rank, LANES), 1)

    def results(at):
        slot = lax.rem(at, slots)
        start = pl.multiple_of(lax.rem(at, per) * step, step)
        m = first + base + at // per
        return (
            pltpu.make_async_copy(approx_buf.at[slot], approx_hbm.at[m, :, pl.ds(start, step)], sems.at[0, slot]),
            pltpu.make_async_copy(err_buf.at[slot], err_hbm.at[m, :, pl.ds(start, step)], sems.at[1, slot]),
        )

    def q_result(i):
        return pltpu.make_async_copy(q_buf.at[i], q_hbm.at[first + base + i], q_sems.at[i])

    @pl.loop(0, total)
    def _(at):
        i = at // per
        m = base + i
        slot = lax.rem(at, slots)
        start = pl.multiple_of(lax.rem(at, per) * step, step)

        @pl.when(lax.rem(at, per) == 0)
        def _():
            one = sum_ref[m]
            orth = jnp.zeros((rank, rows), F32)
            for j in range(rank):
                weight = jnp.sum(jnp.where(lane == m, inv_ref[j], 0.0), axis=1, keepdims=True)
                orth = orth + weight * one[j : j + 1]
            hi = orth.astype(BF16).astype(F32)
            low = (orth - hi).astype(BF16).astype(F32)
            left[...] = jnp.concatenate([hi, low, hi], axis=0).T.astype(BF16)

        @pl.when(at >= slots)
        def _():
            for copy in results(at - slots):
                copy.wait()

        half = step // 2
        for k in range(2):
            here = pl.ds(start + k * half, half)
            right = jnp.concatenate([q_ref[at * tiles + k * (tiles // 2) + t] for t in range(tiles // 2)], axis=1)
            q_buf[i, :, here] = right
            hi = right.astype(BF16).astype(F32)
            low = (right - hi).astype(BF16).astype(F32)
            terms = jnp.concatenate([hi, hi, low], axis=0).astype(BF16)
            approx = jnp.dot(left[...], terms, preferred_element_type=F32)
            there = slice(k * half, (k + 1) * half)
            approx_buf[slot, :, there] = approx
            merged = both_ref[m, :rows, here].astype(F32) + both_ref[m, rows:, here].astype(F32)
            err_buf[slot, :, there] = (merged - approx).astype(BF16)
        for copy in results(at):
            copy.start()

        @pl.when(lax.rem(at, per) == per - 1)
        def _():
            q_result(i).start()

    @pl.loop(max(0, total - slots), total)
    def _(at):
        for copy in results(at):
            copy.wait()

    for i in range(count // 2):
        q_result(i).wait()


VMEM = pl.BlockSpec(memory_space=pltpu.VMEM)
HBM = pl.BlockSpec(memory_space=pltpu.HBM)
SMEM = pl.BlockSpec(memory_space=pltpu.SMEM)
ANY = pl.BlockSpec(memory_space=pl.ANY)
CHUNKS = 2
SLOTS = 6
OUT_STEP = 2048


def limit(mib):
    return pltpu.CompilerParams(vmem_limit_bytes=mib * MIB)


def cost(moved):
    return pl.CostEstimate(flops=0, bytes_accessed=moved, transcendentals=0)


def ordered(kernel, count):
    def call(*refs):
        kernel(*refs[count:])

    return call


def on_device(sizes, grad, error, q_prev):
    groups, shards = sizes
    _, layers, pair, rows, width = grad.shape
    matrices = layers * pair
    rank = q_prev.shape[2]
    pieces = groups * shards
    whole = (matrices, rows, width)
    count = matrices // CHUNKS
    half = count // 2 * width // LANES

    def powers(size):
        return [1 << k for k in range(size.bit_length() - 1)]

    chips = [("shard", k) for k in powers(shards) if k > 1]
    lines = [("dp", k) for k in powers(groups)]
    orders = [[("shard", 1)] + (chips[::-1] if c % 2 else chips) + lines for c in range(CHUNKS)]

    def member(name, step):
        return lax.rem(lax.axis_index(name) // step, 2)

    def place(order):
        at = jnp.int32(0)
        for name, step in order:
            at = at * 2 + member(name, step)
        return at

    sides = {line: member(*line).reshape(1) for line in orders[0]}
    places = [place(order).reshape(1) for order in orders]
    core = sides["shard", 1]

    grads, errors, basis = [
        pltpu.with_memory_space_constraint(x, pltpu.HBM)
        for x in (grad.reshape(whole), error.reshape(whole), q_prev.reshape(matrices, rank, width))
    ]

    def tiled(*shape):
        return jax.ShapeDtypeStruct(shape + (rank, LANES), F32)

    def swap(x, name, step):
        return lax.ppermute(x, name, [(i, i ^ step) for i in range(sizes[0] if name == "dp" else sizes[1])])

    latest = list(sides.values()) + places

    def call(kernel, out_shape, at, *args, name, mib=12, moved=0, scratch=(), spaces=None, out_spaces=None, aliases=None):
        after = list(latest)
        ahead = len(after) + (at is not None)
        outs = pl.pallas_call(
            ordered(kernel, len(after)),
            out_shape=out_shape,
            in_specs=[ANY] * len(after) + [SMEM] * (at is not None) + list(spaces or [VMEM] * len(args)),
            out_specs=out_spaces or jax.tree.map(lambda _: VMEM, out_shape),
            scratch_shapes=list(scratch),
            input_output_aliases={ahead + k: v for k, v in (aliases or {}).items()},
            compiler_params=limit(mib),
            cost_estimate=cost(moved),
            name=name,
        )(*after, *([at] if at is not None else []), *args)
        last = outs[-1] if isinstance(outs, (tuple, list)) else outs
        latest[:] = [last]
        return outs

    p_shape = jax.ShapeDtypeStruct((count, rank, rows), F32)
    boths, owns = [], []
    for c in range(CHUNKS):
        both, own = call(
            functools.partial(left_kernel, first=c * count),
            (pltpu.VMEM((count, 2 * rows, width), BF16), p_shape),
            None, grads, errors, basis,
            name="left", mib=12, moved=count * rows * width, spaces=[HBM] * 3,
            scratch=[pltpu.VMEM((count, rank, width), F32), pltpu.SemaphoreType.DMA((3, count))],
        )
        boths.append(pltpu.with_memory_space_constraint(both, pltpu.VMEM))
        owns.append([own, swap(own, *lines[0])])
    for line in lines[1:]:
        for c in range(CHUNKS):
            own = call(add_kernel, p_shape, None, *owns[c], name="add")
            owns[c] = [own, swap(own, *line)]
    sums, kept = [], []
    for c in range(CHUNKS):
        keep, send, p_sum = call(
            lambda at, both, *refs: right_kernel(at, both, *refs[:-4], refs[-2], refs[-4], refs[-3], refs[-1]),
            (tiled(half + 1), tiled(half + 1), p_shape),
            core, boths[c], *owns[c],
            name="right", moved=count * rows * width, scratch=[pltpu.VMEM((count, 3 * rank, 2 * rows), BF16)],
        )
        sums.append(p_sum)
        kept.append((keep, swap(send, *orders[c][0])))

    size = half
    grams = [None] * CHUNKS
    for stage in range(1, len(orders[0])):
        size //= 2
        for c in range(CHUNKS):
            name, step = orders[c][stage]
            with_gram = name == "shard"
            shape = (tiled(size + with_gram),) * 2
            if orders[c][stage - 1][0] == "shard" and not with_gram:
                shape += (tiled(),)
            outs = call(
                fold_kernel, shape, sides[name, step], *kept[c], name="fold"
            )
            if len(outs) == 3:
                grams[c] = outs[2]
            kept[c] = (outs[0], swap(outs[1], name, step))
    ready, inverses = [], []
    for c in range(CHUNKS):
        piece, inverse = call(
            functools.partial(piece_kernel, per=pieces // count, groups=groups, matrices=count),
            (tiled(size), tiled(rank)),
            places[c], grams[c], *kept[c], name="piece",
        )
        inverses.append(inverse)
        ready.append((piece, swap(piece, *orders[c][-1])))

    def join(c, stage):
        mine = call(
            join_kernel, tiled(2 * ready[c][0].shape[0]), sides[orders[c][stage]], *ready[c], name="join",
        )
        ready[c] = (mine, swap(mine, *orders[c][stage - 1]))

    for stage in range(len(orders[0]) - 1, 1, -1):
        for c in range(CHUNKS):
            join(c, stage)
    results = []
    for c in range(CHUNKS):
        join(c, 1)
        for flip in range(2):
            *results, token = call(
                functools.partial(out_kernel, first=c * count, flip=flip),
                (
                    jax.ShapeDtypeStruct(whole, BF16),
                    jax.ShapeDtypeStruct(whole, F32),
                    jax.ShapeDtypeStruct((matrices, rank, width), F32),
                    tiled(),
                ),
                core, boths[c], sums[c], inverses[c], ready[c][flip], *results,
                name="out", moved=count * rows * width,
                spaces=[VMEM] * 4 + [HBM] * len(results), out_spaces=(HBM, HBM, HBM, VMEM),
                aliases={4 + k: k for k in range(len(results))},
                scratch=[
                    pltpu.VMEM((count // 2, rank, width), F32),
                    pltpu.VMEM((SLOTS, rows, OUT_STEP), BF16),
                    pltpu.VMEM((SLOTS, rows, OUT_STEP), F32),
                    pltpu.VMEM((rows, 3 * rank), BF16),
                    pltpu.SemaphoreType.DMA((2, SLOTS)),
                    pltpu.SemaphoreType.DMA((count // 2,)),
                ],
            )
    error_out, approx, q_new = results
    return error_out.reshape(grad.shape), approx.reshape(layers, pair, rows, width), q_new.reshape(q_prev.shape)


def solution(mesh):
    sizes = (mesh.shape["dp"], mesh.shape["shard"])
    in_specs = (P("dp", None, None, "shard", None), P("dp", None, None, "shard", None), P())
    out_specs = (P("dp", None, None, "shard", None), P(None, None, "shard", None), P())
    return jax.shard_map(
        functools.partial(on_device, sizes), mesh=mesh, in_specs=in_specs, out_specs=out_specs, check_vma=False
    )
```
